32 devices in a mesh: shot: 2 (over x), slab: 16 (over z, y, core).
Axes of the slice: x: 2, y: 2, z: 4, core: 2. Of those that a mesh axis runs over, the one named last changes fastest.
Arguments:
- background_displacement: float32 [6, 5, 5, 5, 16, 4, 128], P('shot', None, None, None, 'slab'), parts along dimension 0, may hold values from -6 to 6
- background_velocity: float32 [6, 5, 5, 5, 16, 4, 128], P('shot', None, None, None, 'slab'), parts along dimension 0, may hold values from -6 to 6
- born_displacement: float32 [6, 5, 5, 5, 16, 4, 128], P('shot', None, None, None, 'slab'), parts along dimension 0, may hold values from -6 to 6
- born_velocity: float32 [6, 5, 5, 5, 16, 4, 128], P('shot', None, None, None, 'slab'), parts along dimension 0, may hold values from -6 to 6
- lame_first: float32 [5, 5, 5, 16, 4, 128], P(None, None, None, 'slab'), may hold values from 0.5 to 1.5
- lame_shear: float32 [5, 5, 5, 16, 4, 128], P(None, None, None, 'slab'), may hold values from 0.5 to 1.5
- density: float32 [5, 5, 5, 16, 4, 128], P(None, None, None, 'slab'), may hold values from 0.8 to 1.2
- perturbation: bfloat16 [42, 5, 5, 5, 16, 4, 128], P('shot', None, None, None, 'slab'), parts along dimension 0, may hold values from -0.59765625 to 0.59765625
- station_element: int32 [2048], replicated, may hold values from 0 to 8191, as said below
Outputs:
- background_final: float32 [6, 5, 5, 5, 16, 4, 128], P('shot', None, None, None, 'slab'), parts along dimension 0
- born_final: float32 [6, 5, 5, 5, 16, 4, 128], P('shot', None, None, None, 'slab'), parts along dimension 0
- station_traces: float32 [6, 20, 2048], P('shot', None, 'slab'), parts along dimension 0
The draws below stay inside these ranges and needn't reach their ends.
There are 2 independent parts, one for each index of `shot`. The reference program is written for one: setup_inputs(seed, part) draws one part's arguments, and reference() takes and returns one part's arrays. A program takes and returns all parts, laid end to end along the dimension named above; an argument that names none is the same for every part. Nothing has to cross between parts.
Inputs may be any that keep to these rules, and one draw needn't show every extreme that they name: `station_element`: each station's element number.
All inputs are finite; a program needn't handle non-finite values.
Results may differ from the reference program's by a relative error of at most 0.0003.
Values sent between devices are 32-bit elements; how exact they have to be, the bound alone decides.
A program may use at most 128 MiB of HBM per device.

```python
import jax
import jax.numpy as jnp
import numpy as np
from jax import lax

NGLL = 5
STEPS = 20
EX = 1
EY = 4
EZ = 128
STA_DEV = 128
NEX = 16
N_SLAB = 16


def draw_station_element(key, part):
    key = jax.random.fold_in(key, 11)
    key_band, key_wide, key_pick, key_cross, key_depth, key_start = jax.random.split(key, 6)
    total_x = EX * N_SLAB
    stations = STA_DEV * N_SLAB
    band_width = max(total_x // 8, 1)
    band_start = jax.random.randint(key_start, (), 0, total_x - band_width + 1)
    crowded = band_start + jax.random.randint(key_band, (stations,), 0, band_width)
    spread = jax.random.randint(key_wide, (stations,), 0, total_x)
    choose = jax.random.randint(key_pick, (stations,), 0, 2)
    along_x = jnp.where(choose == 1, crowded, spread)
    along_y = jax.random.randint(key_cross, (stations,), 0, EY)
    along_z = jax.random.randint(key_depth, (stations,), 0, EZ)
    elements = (along_x * EY + along_y) * EZ + along_z
    elements = elements.at[0].set(0).at[stations - 1].set(total_x * EY * EZ - 1)
    return elements.astype(jnp.int32)


def block_scale(stream_key, dims, cuts, smallest, top_value):
    def one(position, blocks):
        steps = jax.random.uniform(jax.random.fold_in(jax.random.fold_in(stream_key, 6), position), (blocks,), jnp.float32, smallest / len(cuts), top_value / len(cuts))
        return jnp.repeat(jnp.exp(steps), dims[position] // blocks).reshape((-1,) + (1,) * (len(dims) - position - 1))

    factor_of = one(*cuts[0])
    for cut in cuts[1:]:
        factor_of = factor_of * one(*cut)
    return factor_of


def bell_draw(stream_key, dims, scale, reach, cuts=(), held_as=jnp.bfloat16):
    entries = scale * jax.random.normal(stream_key, dims, jnp.float32)
    if cuts:
        entries = entries * block_scale(stream_key, dims, cuts, -0.22, 0.18)
    return jnp.clip(entries, -reach, reach).astype(held_as)


def setup_inputs(seed: int = 0, part: int = 0) -> dict:
    splits = jax.random.split(jax.random.key(seed), 10)
    part_keys = jax.random.split(jax.random.fold_in(splits[9], part), 10)
    background_displacement = bell_draw(part_keys[0], (3, NGLL, NGLL, NGLL, NEX, EY, EZ), 1.0, 6.0, ((4, 16),), jnp.float32)
    background_velocity = bell_draw(part_keys[1], (3, NGLL, NGLL, NGLL, NEX, EY, EZ), 1.0, 6.0, ((4, 16),), jnp.float32)
    born_displacement = bell_draw(part_keys[2], (3, NGLL, NGLL, NGLL, NEX, EY, EZ), 1.0, 6.0, ((4, 16),), jnp.float32)
    born_velocity = bell_draw(part_keys[3], (3, NGLL, NGLL, NGLL, NEX, EY, EZ), 1.0, 6.0, ((4, 16),), jnp.float32)
    lame_first = jnp.clip(0.5 + 1.0 * jax.random.uniform(splits[4], (NGLL, NGLL, NGLL, NEX, EY, EZ), jnp.float32) ** block_scale(splits[4], (NGLL, NGLL, NGLL, NEX, EY, EZ), ((3, 16),), -0.2, 0.2), 0.5, 1.5)
    lame_shear = jnp.clip(0.5 + 1.0 * jax.random.uniform(splits[5], (NGLL, NGLL, NGLL, NEX, EY, EZ), jnp.float32) ** block_scale(splits[5], (NGLL, NGLL, NGLL, NEX, EY, EZ), ((3, 16),), -0.2, 0.2), 0.5, 1.5)
    density = jnp.clip(0.8 + 0.40000004 * jax.random.uniform(splits[6], (NGLL, NGLL, NGLL, NEX, EY, EZ), jnp.float32) ** block_scale(splits[6], (NGLL, NGLL, NGLL, NEX, EY, EZ), ((3, 16),), -0.2, 0.2), 0.8, 1.2)
    perturbation = bell_draw(part_keys[7], (21, NGLL, NGLL, NGLL, NEX, EY, EZ), 0.1, 0.59765625, ((4, 16),))
    station_element = draw_station_element(jax.random.fold_in(splits[9], 71), part)
    return {"background_displacement": background_displacement, "background_velocity": background_velocity, "born_displacement": born_displacement, "born_velocity": born_velocity, "lame_first": lame_first, "lame_shear": lame_shear, "density": density, "perturbation": perturbation, "station_element": station_element}


HIGH = lax.Precision.HIGHEST
time_step = 0.02
VOIGT_PAIRS = ((0, 0), (0, 1), (0, 2), (0, 3), (0, 4), (0, 5), (1, 1), (1, 2), (1, 3), (1, 4), (1, 5), (2, 2), (2, 3), (2, 4), (2, 5), (3, 3), (3, 4), (3, 5), (4, 4), (4, 5), (5, 5))

def gll_tables():
    points = np.array([-1.0, -np.sqrt(3.0 / 7.0), 0.0, np.sqrt(3.0 / 7.0), 1.0])
    weights = np.array([0.1, 49.0 / 90.0, 32.0 / 45.0, 49.0 / 90.0, 0.1])
    derivative = np.zeros((5, 5))
    for node_at in range(5):
        for node_of in range(5):
            if node_at == node_of:
                derivative[node_at, node_of] = sum((1.0 / (points[node_at] - points[another]) for another in range(5) if another != node_at))
            else:
                upper_part = np.prod([points[node_at] - points[another] for another in range(5) if another != node_at])
                lower_part = np.prod([points[node_of] - points[another] for another in range(5) if another != node_of])
                derivative[node_at, node_of] = upper_part / lower_part / (points[node_at] - points[node_of])
    weight_cube = weights[:, None, None] * weights[None, :, None] * weights[None, None, :]
    return (jnp.asarray(derivative, jnp.float32), jnp.asarray(weight_cube, jnp.float32))

def strains(field_in, derivative):
    grad_x = jnp.einsum('im,cmjkxyz->cijkxyz', derivative, field_in, precision=HIGH)
    grad_y = jnp.einsum('jm,cimkxyz->cijkxyz', derivative, field_in, precision=HIGH)
    grad_z = jnp.einsum('km,cijmxyz->cijkxyz', derivative, field_in, precision=HIGH)
    return [grad_x[0], grad_y[1], grad_z[2], grad_y[2] + grad_z[1], grad_x[2] + grad_z[0], grad_x[1] + grad_y[0]]

def isotropic(strain_list, lame_first, lame_shear):
    dilation = strain_list[0] + strain_list[1] + strain_list[2]
    normal_part = [lame_first * dilation + 2.0 * lame_shear * strain_list[voigt_id] for voigt_id in range(3)]
    return normal_part + [lame_shear * strain_list[voigt_id] for voigt_id in range(3, 6)]

def anisotropic(perturbation, strain_list):
    extra = [jnp.zeros_like(strain_list[0]) for voigt_id in range(6)]
    for pair_id, (row_id, col_id) in enumerate(VOIGT_PAIRS):
        coefficient = perturbation[pair_id].astype(jnp.float32)
        extra[row_id] = extra[row_id] + coefficient * strain_list[col_id]
        if row_id != col_id:
            extra[col_id] = extra[col_id] + coefficient * strain_list[row_id]
    return extra

def apply_x(derivative, values):
    return jnp.einsum('mi,mjkxyz->ijkxyz', derivative, values, precision=HIGH)

def apply_y(derivative, values):
    return jnp.einsum('mj,imkxyz->ijkxyz', derivative, values, precision=HIGH)

def apply_z(derivative, values):
    return jnp.einsum('mk,ijmxyz->ijkxyz', derivative, values, precision=HIGH)

def forces(stress, derivative, weight_cube):
    scaled = [weight_cube[:, :, :, None, None, None] * component for component in stress]
    stress_xx, stress_yy, stress_zz, stress_yz, stress_xz, stress_xy = scaled
    force_x = -(apply_x(derivative, stress_xx) + apply_y(derivative, stress_xy) + apply_z(derivative, stress_xz))
    force_y = -(apply_x(derivative, stress_xy) + apply_y(derivative, stress_yy) + apply_z(derivative, stress_yz))
    force_z = -(apply_x(derivative, stress_xz) + apply_y(derivative, stress_yz) + apply_z(derivative, stress_zz))
    return jnp.stack([force_x, force_y, force_z])

def pair_faces(first_face, last_face, element_dim):
    length = first_face.shape[element_dim]
    zero_face = jnp.zeros_like(lax.slice_in_dim(first_face, 0, 1, axis=element_dim))
    next_first = jnp.concatenate([lax.slice_in_dim(first_face, 1, length, axis=element_dim), zero_face], element_dim)
    prev_last = jnp.concatenate([zero_face, lax.slice_in_dim(last_face, 0, length - 1, axis=element_dim)], element_dim)
    return (first_face + prev_last, last_face + next_first)

def assemble_dim(values, node_dim, element_dim):
    first_face = lax.index_in_dim(values, 0, node_dim, keepdims=False)
    last_face = lax.index_in_dim(values, 4, node_dim, keepdims=False)
    new_first, new_last = pair_faces(first_face, last_face, element_dim - 1)
    middle = lax.slice_in_dim(values, 1, 4, axis=node_dim)
    return jnp.concatenate([jnp.expand_dims(new_first, node_dim), middle, jnp.expand_dims(new_last, node_dim)], node_dim)

def assemble_whole(values):
    values = assemble_dim(values, 1, 4)
    values = assemble_dim(values, 2, 5)
    return assemble_dim(values, 3, 6)

def reference(background_displacement, background_velocity, born_displacement, born_velocity, lame_first, lame_shear, density, perturbation, station_element):
    derivative, weight_cube = gll_tables()
    nodal_mass = weight_cube[:, :, :, None, None, None] * density
    stacked = jnp.concatenate([background_displacement, background_velocity, born_displacement, born_velocity, nodal_mass[None], jnp.ones_like(nodal_mass)[None]], 0)
    shared = assemble_whole(stacked)
    copies = shared[13]
    assembled_mass = shared[12]
    fields = shared[:12] / copies
    back_disp, back_velo, born_disp, born_velo = (fields[0:3], fields[3:6], fields[6:9], fields[9:12])
    samples = []
    for step_id in range(STEPS):
        back_strain = strains(back_disp, derivative)
        saved_strain = [lax.optimization_barrier(component.astype(jnp.bfloat16)).astype(jnp.float32) for component in back_strain]
        back_force = forces(isotropic(back_strain, lame_first, lame_shear), derivative, weight_cube)
        born_stress = isotropic(strains(born_disp, derivative), lame_first, lame_shear)
        extra = anisotropic(perturbation, saved_strain)
        born_stress = [first_term + second_term for first_term, second_term in zip(born_stress, extra)]
        born_force = forces(born_stress, derivative, weight_cube)
        both_forces = assemble_whole(jnp.concatenate([back_force, born_force], 0))
        back_velo = back_velo + time_step * both_forces[:3] / assembled_mass
        back_disp = back_disp + time_step * back_velo
        born_velo = born_velo + time_step * both_forces[3:] / assembled_mass
        born_disp = born_disp + time_step * born_velo
        centers = born_disp[:, 2, 2, 2].reshape(3, -1)
        samples.append(jnp.take(centers, station_element, axis=1))
    return (back_disp, born_disp, jnp.stack(samples, 1))
```

```python
import jax
import jax.numpy as jnp
import numpy as np
from jax import lax
from jax.experimental import pallas as pl
from jax.experimental.pallas import tpu as pltpu
from jax.sharding import PartitionSpec as P

STEPS = 20
HIGH = lax.Precision.HIGHEST
MESH = pl.DeviceIdType.MESH
time_step = 0.02
PAIR = {}
for _row in range(6):
    for _col in range(_row, 6):
        PAIR[_row, _col] = PAIR[_col, _row] = len(set(PAIR.values()))


def gll_tables():
    points = np.array([-1.0, -np.sqrt(3.0 / 7.0), 0.0, np.sqrt(3.0 / 7.0), 1.0])
    weights = np.array([0.1, 49.0 / 90.0, 32.0 / 45.0, 49.0 / 90.0, 0.1])
    derivative = np.zeros((5, 5))
    for node_at in range(5):
        for node_of in range(5):
            if node_at == node_of:
                derivative[node_at, node_of] = sum(
                    (
                        1.0 / (points[node_at] - points[another])
                        for another in range(5)
                        if another != node_at
                    )
                )
            else:
                upper_part = np.prod(
                    [
                        points[node_at] - points[another]
                        for another in range(5)
                        if another != node_at
                    ]
                )
                lower_part = np.prod(
                    [
                        points[node_of] - points[another]
                        for another in range(5)
                        if another != node_of
                    ]
                )
                derivative[node_at, node_of] = (
                    upper_part / lower_part / (points[node_at] - points[node_of])
                )
    weight_cube = weights[:, None, None] * weights[None, :, None] * weights[None, None, :]
    return (derivative, weight_cube)


DERIV, WEIGHT = gll_tables()


def apply5(matrix, u):
    m = [[float(x) for x in row] for row in matrix]
    d1, d2, s1, s2 = u[0] - u[4], u[1] - u[3], u[0] + u[4], u[1] + u[3]
    e0 = 0.5 * (m[0][0] - m[0][4]) * d1 + 0.5 * (m[0][1] - m[0][3]) * d2
    e1 = 0.5 * (m[1][0] - m[1][4]) * d1 + 0.5 * (m[1][1] - m[1][3]) * d2
    o0 = 0.5 * (m[0][0] + m[0][4]) * s1 + 0.5 * (m[0][1] + m[0][3]) * s2 + m[0][2] * u[2]
    o1 = 0.5 * (m[1][0] + m[1][4]) * s1 + 0.5 * (m[1][1] + m[1][3]) * s2 + m[1][2] * u[2]
    return [e0 + o0, e1 + o1, m[2][0] * d1 + m[2][1] * d2, e1 - o1, e0 - o0]


def forward(u):
    return apply5(DERIV, u)


def backward(u):
    return apply5(DERIV.T, u)


def assemble_plane(rows, average=False):
    shape = rows[0].shape
    y_elem = lax.broadcasted_iota(jnp.int32, shape, 1) % 4
    z_elem = lax.broadcasted_iota(jnp.int32, shape[1:], 1)
    last_z = shape[2] - 1
    first = rows[0] + jnp.where(y_elem > 0, pltpu.roll(rows[4], 1, 1), 0.0)
    last = rows[4] + jnp.where(y_elem < 3, pltpu.roll(rows[0], 7, 1), 0.0)
    if average:
        first = first * jnp.where(y_elem > 0, 0.5, 1.0)
        last = last * jnp.where(y_elem < 3, 0.5, 1.0)
    rows = [first, rows[1], rows[2], rows[3], last]
    out = []
    for row in rows:
        low = row[0] + jnp.where(z_elem > 0, pltpu.roll(row[4], 1, 1), 0.0)
        high = row[4] + jnp.where(z_elem < last_z, pltpu.roll(row[0], last_z, 1), 0.0)
        if average:
            low = low * jnp.where(z_elem > 0, 0.5, 1.0)
            high = high * jnp.where(z_elem < last_z, 0.5, 1.0)
        out.append([low, row[1], row[2], row[3], high])
    return out


def kernel(
    count, disp_in, velo_in, mass_in, lam, shear, pert,
    disp, records,
    velo, rate, grad_x, grad_y, stress, force, faces, first_faces,
    send_sem, recv_sem, first_send, first_recv,
):
    me = lax.axis_index("slab")
    has = (me > 0, me < count - 1)
    beside = (jnp.maximum(me - 1, 0), jnp.minimum(me + 1, count - 1))
    side_plane = (0, 4)

    barrier = pltpu.get_barrier_semaphore()
    for side in range(2):
        @pl.when(has[side])
        def _(side=side):
            pl.semaphore_signal(
                barrier, inc=1, device_id={"slab": beside[side]}, device_id_type=MESH
            )

        @pl.when(jnp.logical_not(has[side]))
        def _(side=side):
            faces[0, side] = jnp.zeros_like(faces[0, side])
            faces[1, side] = jnp.zeros_like(faces[1, side])
            first_faces[side] = jnp.zeros_like(first_faces[side])

    def tidy_first(source, target, average):
        def one(i, carry):
            out = assemble_plane([source[i, j] for j in range(5)], average)
            for j in range(5):
                for k in range(5):
                    target[i, j, k] = out[j][k]
            return carry
        lax.fori_loop(0, 5, one, 0)

    for c in range(3):
        tidy_first(disp_in.at[c], disp.at[c], True)
        tidy_first(velo_in.at[c], velo.at[c], True)
    tidy_first(mass_in, rate, False)

    pl.semaphore_wait(barrier, has[0].astype(jnp.int32) + has[1].astype(jnp.int32))

    starts = [disp.at[c] for c in range(3)] + [velo.at[c] for c in range(3)] + [rate]

    def first_copy(side, item):
        return pltpu.make_async_remote_copy(
            src_ref=starts[item].at[side_plane[side]],
            dst_ref=first_faces.at[1 - side, item],
            send_sem=first_send.at[side, item],
            recv_sem=first_recv.at[1 - side, item],
            device_id={"slab": beside[side]},
            device_id_type=MESH,
        )

    def first_arrival(side, item):
        return pltpu.make_async_remote_copy(
            src_ref=starts[item].at[side_plane[side]],
            dst_ref=first_faces.at[side, item],
            send_sem=first_send.at[side, item],
            recv_sem=first_recv.at[side, item],
            device_id={"slab": beside[side]},
            device_id_type=MESH,
        )

    for side in range(2):
        @pl.when(has[side])
        def _(side=side):
            for item in range(7):
                first_copy(side, item).start()
    for side in range(2):
        @pl.when(has[side])
        def _(side=side):
            for item in range(7):
                first_arrival(side, item).wait()

    for side in range(2):
        i = side_plane[side]
        scale = jnp.where(has[side], 0.5, 1.0).astype(jnp.float32)
        for item in range(7):
            def add_first(j, carry, side=side, i=i, item=item, scale=scale):
                total = starts[item][i, j] + first_faces[side, item, j]
                starts[item][i, j] = total * scale if item < 6 else total
                return carry
            lax.fori_loop(0, 5, add_first, 0)

    def invert(i, carry):
        for j in range(5):
            rate[i, j] = -time_step / rate[i, j]
        return carry
    lax.fori_loop(0, 5, invert, 0)

    def along_y(i):
        def one(c, carry):
            out = forward([disp[c, i, j] for j in range(5)])
            for j in range(5):
                grad_y[c, i, j] = out[j]
            return carry
        lax.fori_loop(0, 3, one, 0)

    def all_along_y(i, carry):
        along_y(i)
        return carry
    lax.fori_loop(0, 5, all_along_y, 0)

    def move(c, i, j, total):
        new_velo = velo[c, i, j] + total * rate[i, j]
        velo[c, i, j] = new_velo
        disp[c, i, j] = disp[c, i, j] + time_step * new_velo

    def copy_out(slot, side, c):
        return pltpu.make_async_remote_copy(
            src_ref=force.at[c, side_plane[side]],
            dst_ref=faces.at[slot, 1 - side, c],
            send_sem=send_sem.at[side, c],
            recv_sem=recv_sem.at[slot, 1 - side, c],
            device_id={"slab": beside[side]},
            device_id_type=MESH,
        )

    def copy_in(slot, side, c):
        return pltpu.make_async_remote_copy(
            src_ref=force.at[c, side_plane[side]],
            dst_ref=faces.at[slot, side, c],
            send_sem=send_sem.at[side, c],
            recv_sem=recv_sem.at[slot, side, c],
            device_id={"slab": beside[side]},
            device_id_type=MESH,
        )

    def step(step_id, carry):
        slot = step_id % 2

        def along_x(line, inner):
            c, j = line // 5, line % 5
            out = forward([disp[c, i, j] for i in range(5)])
            for i in range(5):
                grad_x[c, i, j] = out[i]
            return inner
        lax.fori_loop(0, 15, along_x, 0)

        def stresses(line, inner):
            i, j = line // 5, line % 5
            gz = []
            for c in range(3):
                row = disp[c, i, j]
                gz.append(jnp.stack(forward([row[k] for k in range(5)])))
            strain = [
                grad_x[0, i, j],
                grad_y[1, i, j],
                gz[2],
                grad_y[2, i, j] + gz[1],
                grad_x[2, i, j] + gz[0],
                grad_x[1, i, j] + grad_y[0, i, j],
            ]
            shear_here = shear[i, j]
            twice = shear_here + shear_here
            spread = lam[i, j] * (strain[0] + strain[1] + strain[2])
            out = [spread + twice * strain[v] for v in range(3)]
            out += [shear_here * strain[v] for v in range(3, 6)]
            saved = [
                pltpu.roll(s.astype(jnp.bfloat16).astype(jnp.float32), 4, 1) for s in strain
            ]
            for v in range(6):
                for w in range(6):
                    out[v] = out[v] + pert[PAIR[v, w], i, j] * saved[w]
            s_xx, s_yy, s_zz, s_yz, s_xz, s_xy = out
            for c, value in enumerate((s_xz, s_yz, s_zz)):
                done = backward([value[k] for k in range(5)])
                for k in range(5):
                    force[c, i, j, k] = done[k]
            for place, value in enumerate((s_xx, s_xy, s_xz, s_yy, s_yz)):
                stress[place, i, j] = value
            return inner
        lax.fori_loop(0, 25, stresses, 0)

        for c in range(3):
            x_place, y_place = (0, 1, 2)[c], (1, 3, 4)[c]

            def force_y(i, inner, c=c, y_place=y_place):
                out = backward([stress[y_place, i, j] for j in range(5)])
                for j in range(5):
                    force[c, i, j] = force[c, i, j] + out[j]
                return inner
            lax.fori_loop(0, 5, force_y, 0)

            def force_x(j, inner, c=c, x_place=x_place):
                out = backward([stress[x_place, i, j] for i in range(5)])
                for i in range(5):
                    force[c, i, j] = force[c, i, j] + out[i]
                return inner
            lax.fori_loop(0, 5, force_x, 0)

            for side in range(2):
                i = side_plane[side]
                out = assemble_plane([force[c, i, j] for j in range(5)])
                for j in range(5):
                    for k in range(5):
                        force[c, i, j, k] = out[j][k]

                @pl.when(has[side])
                def _(side=side, c=c):
                    copy_out(slot, side, c).start()

        def inside(line, inner):
            c, i = line // 3, 1 + line % 3
            out = assemble_plane([force[c, i, j] for j in range(5)])
            for j in range(5):
                move(c, i, j, jnp.stack(out[j]))
            return inner
        lax.fori_loop(0, 9, inside, 0)

        def inside_y(i, inner):
            along_y(i)
            return inner
        lax.fori_loop(1, 4, inside_y, 0)

        for side in range(2):
            @pl.when(has[side])
            def _(side=side):
                for c in range(3):
                    copy_in(slot, side, c).wait()

            def outside(c, inner, side=side):
                i = side_plane[side]
                for j in range(5):
                    move(c, i, j, force[c, i, j] + faces[slot, side, c, j])
                return inner
            lax.fori_loop(0, 3, outside, 0)
            along_y(side_plane[side])

        for c in range(3):
            records[step_id, c] = disp[c, 2, 2, 2]
        return carry

    lax.fori_loop(0, STEPS, step, 0)


def on_device(
    background_displacement,
    background_velocity,
    born_displacement,
    born_velocity,
    lame_first,
    lame_shear,
    density,
    perturbation,
    station_element,
):
    count = lax.axis_size("slab")
    y_count, z_count = density.shape[4:]
    weight = jnp.asarray(WEIGHT, jnp.float32)[:, :, :, None, None]

    def both(first, second):
        return jnp.concatenate([first, second], axis=-2)

    disp_in = both(background_displacement[:, :, :, :, 0], born_displacement[:, :, :, :, 0])
    velo_in = both(background_velocity[:, :, :, :, 0], born_velocity[:, :, :, :, 0])
    mass, lam, shear = [weight * a[:, :, :, 0] for a in (density, lame_first, lame_shear)]
    mass, lam, shear = both(mass, mass), both(lam, lam), both(shear, shear)
    pert = weight * perturbation[:, :, :, :, 0].astype(jnp.float32)
    pert = both(jnp.zeros_like(pert), pert)

    cube = (5, 5, 5, 2 * y_count, z_count)
    face = (5, 5, 2 * y_count, z_count)
    vmem = pl.BlockSpec(memory_space=pltpu.VMEM)
    disp, records = pl.pallas_call(
        lambda *refs: kernel(count, *refs),
        out_shape=(
            jax.ShapeDtypeStruct((3,) + cube, jnp.float32),
            jax.ShapeDtypeStruct((STEPS, 3) + cube[3:], jnp.float32),
        ),
        in_specs=[vmem] * 6,
        out_specs=(vmem, vmem),
        scratch_shapes=[
            pltpu.VMEM((3,) + cube, jnp.float32),
            pltpu.VMEM(cube, jnp.float32),
            pltpu.VMEM((3,) + cube, jnp.float32),
            pltpu.VMEM((3,) + cube, jnp.float32),
            pltpu.VMEM((5,) + cube, jnp.float32),
            pltpu.VMEM((3,) + cube, jnp.float32),
            pltpu.VMEM((2, 2, 3) + face, jnp.float32),
            pltpu.VMEM((2, 7) + face, jnp.float32),
            pltpu.SemaphoreType.DMA((2, 3)),
            pltpu.SemaphoreType.DMA((2, 2, 3)),
            pltpu.SemaphoreType.DMA((2, 7)),
            pltpu.SemaphoreType.DMA((2, 7)),
        ],
        compiler_params=pltpu.CompilerParams(
            collective_id=0, has_side_effects=True, vmem_limit_bytes=56 * 1024 * 1024
        ),
        name="born_window",
    )(disp_in, velo_in, mass, lam, shear, pert)

    back_disp = disp[:, :, :, :, None, :y_count]
    born_disp = disp[:, :, :, :, None, y_count:]
    elements_here = y_count * z_count
    rows = records[:, :, y_count:].reshape(STEPS * 3, elements_here)
    owned_count = station_element.shape[0] // count
    owned_ids = lax.dynamic_slice_in_dim(
        station_element, lax.axis_index("slab") * owned_count, owned_count
    )
    gathered = lax.all_gather(rows, "slab", axis=0)
    element_ids = jnp.arange(count * elements_here, dtype=jnp.int32)
    chosen = (element_ids[:, None] == owned_ids[None, :]).astype(jnp.float32)
    chosen = chosen.reshape(count, elements_here, owned_count)
    picked = jnp.einsum("dre,des->rs", gathered, chosen, precision=HIGH)
    station_traces = picked.reshape(STEPS, 3, owned_count).transpose(1, 0, 2)
    return (back_disp, born_disp, station_traces)


def solution(mesh):
    placed = (
        P("shot", None, None, None, "slab", None, None),
        P("shot", None, None, None, "slab", None, None),
        P("shot", None, None, None, "slab", None, None),
        P("shot", None, None, None, "slab", None, None),
        P(None, None, None, "slab", None, None),
        P(None, None, None, "slab", None, None),
        P(None, None, None, "slab", None, None),
        P("shot", None, None, None, "slab", None, None),
        P(),
    )
    return jax.shard_map(
        on_device,
        mesh=mesh,
        in_specs=placed,
        out_specs=(
            P("shot", None, None, None, "slab", None, None),
            P("shot", None, None, None, "slab", None, None),
            P("shot", None, "slab"),
        ),
        check_vma=False,
    )
```

```python
import jax
import jax.numpy as jnp
import numpy as np
from jax import lax
from jax.experimental import pallas as pl
from jax.experimental.pallas import tpu as pltpu
from jax.sharding import PartitionSpec as P

STEPS = 20
HIGH = lax.Precision.HIGHEST
MESH = pl.DeviceIdType.MESH
time_step = 0.02
PAIR = {}
for _row in range(6):
    for _col in range(_row, 6):
        PAIR[_row, _col] = PAIR[_col, _row] = len(set(PAIR.values()))


def gll_tables():
    points = np.array([-1.0, -np.sqrt(3.0 / 7.0), 0.0, np.sqrt(3.0 / 7.0), 1.0])
    weights = np.array([0.1, 49.0 / 90.0, 32.0 / 45.0, 49.0 / 90.0, 0.1])
    derivative = np.zeros((5, 5))
    for node_at in range(5):
        for node_of in range(5):
            if node_at == node_of:
                derivative[node_at, node_of] = sum(
                    (
                        1.0 / (points[node_at] - points[another])
                        for another in range(5)
                        if another != node_at
                    )
                )
            else:
                upper_part = np.prod(
                    [
                        points[node_at] - points[another]
                        for another in range(5)
                        if another != node_at
                    ]
                )
                lower_part = np.prod(
                    [
                        points[node_of] - points[another]
                        for another in range(5)
                        if another != node_of
                    ]
                )
                derivative[node_at, node_of] = (
                    upper_part / lower_part / (points[node_at] - points[node_of])
                )
    weight_cube = weights[:, None, None] * weights[None, :, None] * weights[None, None, :]
    return (derivative, weight_cube)


DERIV, WEIGHT = gll_tables()


def apply5(matrix, u):
    m = [[float(x) for x in row] for row in matrix]
    d1, d2, s1, s2 = u[0] - u[4], u[1] - u[3], u[0] + u[4], u[1] + u[3]
    e0 = 0.5 * (m[0][0] - m[0][4]) * d1 + 0.5 * (m[0][1] - m[0][3]) * d2
    e1 = 0.5 * (m[1][0] - m[1][4]) * d1 + 0.5 * (m[1][1] - m[1][3]) * d2
    o0 = 0.5 * (m[0][0] + m[0][4]) * s1 + 0.5 * (m[0][1] + m[0][3]) * s2 + m[0][2] * u[2]
    o1 = 0.5 * (m[1][0] + m[1][4]) * s1 + 0.5 * (m[1][1] + m[1][3]) * s2 + m[1][2] * u[2]
    return [e0 + o0, e1 + o1, m[2][0] * d1 + m[2][1] * d2, e1 - o1, e0 - o0]


def forward(u):
    return apply5(DERIV, u)


def backward(u):
    return apply5(DERIV.T, u)


def backward_ends(u):
    out = backward(u)
    return out[0], out[4]


def assemble_y(first, last, average=False):
    y_elem = lax.broadcasted_iota(jnp.int32, first.shape, 1) % 4
    new_first = first + jnp.where(y_elem > 0, pltpu.roll(last, 1, 1), 0.0)
    new_last = last + jnp.where(y_elem < 3, pltpu.roll(first, 7, 1), 0.0)
    if average:
        new_first = new_first * jnp.where(y_elem > 0, 0.5, 1.0)
        new_last = new_last * jnp.where(y_elem < 3, 0.5, 1.0)
    return new_first, new_last


def assemble_z(row, average=False):
    z_elem = lax.broadcasted_iota(jnp.int32, row.shape[1:], 1)
    last_z = row.shape[2] - 1
    low = row[0] + jnp.where(z_elem > 0, pltpu.roll(row[4], 1, 1), 0.0)
    high = row[4] + jnp.where(z_elem < last_z, pltpu.roll(row[0], last_z, 1), 0.0)
    if average:
        low = low * jnp.where(z_elem > 0, 0.5, 1.0)
        high = high * jnp.where(z_elem < last_z, 0.5, 1.0)
    return [low, row[1], row[2], row[3], high]


def assemble_plane(rows, average=False):
    first, last = assemble_y(rows[0], rows[4], average)
    return [assemble_z(row, average) for row in (first, rows[1], rows[2], rows[3], last)]


def kernel(
    count, back_disp, back_velo, born_disp, born_velo, mass_in, lam_in, shear_in, pert, chosen,
    disp, traces,
    velo, rate, lam, shear, grad_x, grad_y, stress, force, rows_out, rims_out,
    rows_in, rims_in, first_faces,
    records, outbox, inbox,
    send_sem, recv_sem, first_send, first_recv, station_send, station_recv,
):
    me = lax.axis_index("slab")
    has = (me > 0, me < count - 1)
    beside = (jnp.maximum(me - 1, 0), jnp.minimum(me + 1, count - 1))
    side_plane = (0, 4)

    barrier = pltpu.get_barrier_semaphore()

    def greet(away, carry):
        pl.semaphore_signal(
            barrier, inc=1, device_id={"slab": (me + away) % count}, device_id_type=MESH
        )
        return carry
    lax.fori_loop(1, count, greet, 0)

    records[...] = jnp.zeros_like(records)
    for side in range(2):
        @pl.when(jnp.logical_not(has[side]))
        def _(side=side):
            for slot in range(2):
                rows_in[slot, side] = jnp.zeros_like(rows_in[slot, side])
                rims_in[slot, side] = jnp.zeros_like(rims_in[slot, side])
            first_faces[side] = jnp.zeros_like(first_faces[side])

    def both(first, second):
        return jnp.concatenate([first, second], axis=1)

    def tidy_first(first, second, target, average):
        def one(i, carry):
            out = assemble_plane([both(first[i, j], second[i, j]) for j in range(5)], average)
            for j in range(5):
                for k in range(5):
                    target[i, j, k] = out[j][k]
            return carry
        lax.fori_loop(0, 5, one, 0)

    for c in range(3):
        tidy_first(back_disp.at[c], born_disp.at[c], disp.at[c], True)
        tidy_first(back_velo.at[c], born_velo.at[c], velo.at[c], True)
    tidy_first(mass_in, mass_in, rate, False)

    def widen(i, carry):
        for j in range(5):
            lam[i, j] = both(lam_in[i, j], lam_in[i, j])
            shear[i, j] = both(shear_in[i, j], shear_in[i, j])
        return carry
    lax.fori_loop(0, 5, widen, 0)

    pl.semaphore_wait(barrier, count - 1)

    starts = [disp.at[c] for c in range(3)] + [velo.at[c] for c in range(3)] + [rate]

    def first_copy(side, item):
        return pltpu.make_async_remote_copy(
            src_ref=starts[item].at[side_plane[side]],
            dst_ref=first_faces.at[1 - side, item],
            send_sem=first_send.at[side, item],
            recv_sem=first_recv.at[1 - side, item],
            device_id={"slab": beside[side]},
            device_id_type=MESH,
        )

    def first_arrival(side, item):
        return pltpu.make_async_remote_copy(
            src_ref=starts[item].at[side_plane[side]],
            dst_ref=first_faces.at[side, item],
            send_sem=first_send.at[side, item],
            recv_sem=first_recv.at[side, item],
            device_id={"slab": beside[side]},
            device_id_type=MESH,
        )

    for side in range(2):
        @pl.when(has[side])
        def _(side=side):
            for item in range(7):
                first_copy(side, item).start()
    for side in range(2):
        @pl.when(has[side])
        def _(side=side):
            for item in range(7):
                first_arrival(side, item).wait()

    for side in range(2):
        i = side_plane[side]
        scale = jnp.where(has[side], 0.5, 1.0).astype(jnp.float32)
        for item in range(7):
            def add_first(j, carry, side=side, i=i, item=item, scale=scale):
                total = starts[item][i, j] + first_faces[side, item, j]
                starts[item][i, j] = total * scale if item < 6 else total
                return carry
            lax.fori_loop(0, 5, add_first, 0)

    def invert(i, carry):
        for j in range(5):
            rate[i, j] = -time_step / rate[i, j]
        return carry
    lax.fori_loop(0, 5, invert, 0)

    def along_y(i):
        def one(c, carry):
            out = forward([disp[c, i, j] for j in range(5)])
            for j in range(5):
                grad_y[c, i, j] = out[j]
            return carry
        lax.fori_loop(0, 3, one, 0)

    def all_along_y(i, carry):
        along_y(i)
        return carry
    lax.fori_loop(0, 5, all_along_y, 0)

    def move(c, i, j, total):
        new_velo = velo[c, i, j] + total * rate[i, j]
        velo[c, i, j] = new_velo
        disp[c, i, j] = disp[c, i, j] + time_step * new_velo

    def face_copy(slot, side, item, landing):
        out, into = (rows_out, rows_in) if item < 4 else (rims_out, rims_in)
        row = (item,) if item < 4 else ()
        return pltpu.make_async_remote_copy(
            src_ref=out.at[(side,) + row],
            dst_ref=into.at[(slot, landing) + row],
            send_sem=send_sem.at[side, item],
            recv_sem=recv_sem.at[slot, landing, item],
            device_id={"slab": beside[side]},
            device_id_type=MESH,
        )

    def send_face(slot, item):
        for side in range(2):
            @pl.when(has[side])
            def _(side=side):
                face_copy(slot, side, item, 1 - side).start()

    tile = disp.shape[4:]
    y_elem = lax.broadcasted_iota(jnp.int32, tile, 0) % 4
    z_elem = lax.broadcasted_iota(jnp.int32, tile, 1)
    last_z = tile[1] - 1

    half = back_disp.shape[4]
    groups, per_group = traces.shape[0], STEPS // traces.shape[0]

    def to_station(group, away):
        return pltpu.make_async_remote_copy(
            src_ref=outbox.at[group, away],
            dst_ref=inbox.at[group, away],
            send_sem=station_send.at[group, away],
            recv_sem=station_recv.at[group, away],
            device_id={"slab": (me + away) % count},
            device_id_type=MESH,
        )

    def send_traces(group):
        rest = jnp.concatenate([records[y] for y in range(half)], axis=1)
        pieces = []
        for _ in range(3):
            pieces.append(rest.astype(jnp.bfloat16))
            rest = rest - pieces[-1].astype(jnp.float32)
        pieces = jnp.concatenate(pieces, axis=0)
        rows = rest.shape[0]

        def pick(away):
            found = jnp.dot(
                pieces, chosen[(me + away) % count], preferred_element_type=jnp.float32
            )
            outbox[group, away] = (
                found[:rows] + found[rows : 2 * rows] + found[2 * rows :]
            )
        pick(0)

        def pick_and_send(away, carry):
            pick(away)
            to_station(group, away).start()
            return carry
        lax.fori_loop(1, count, pick_and_send, 0)

    def step(step_id, carry):
        slot = step_id % 2

        def along_x(line, inner):
            c, j = line // 5, line % 5
            out = forward([disp[c, i, j] for i in range(5)])
            for i in range(5):
                grad_x[c, i, j] = out[i]
            return inner
        lax.fori_loop(0, 15, along_x, 0)

        upper = lax.broadcasted_iota(jnp.int32, tile, 0) < half

        def stresses(i, j):
            gz = []
            for c in range(3):
                row = disp[c, i, j]
                gz.append(jnp.stack(forward([row[k] for k in range(5)])))
            strain = [
                grad_x[0, i, j],
                grad_y[1, i, j],
                gz[2],
                grad_y[2, i, j] + gz[1],
                grad_x[2, i, j] + gz[0],
                grad_x[1, i, j] + grad_y[0, i, j],
            ]
            shear_here = shear[i, j]
            twice = shear_here + shear_here
            spread = lam[i, j] * (strain[0] + strain[1] + strain[2])
            out = [spread + twice * strain[v] for v in range(3)]
            out += [shear_here * strain[v] for v in range(3, 6)]
            saved = []
            for t in strain:
                t = t.astype(jnp.bfloat16).astype(jnp.float32)
                pairs = [
                    jnp.where(upper, t[k], pltpu.roll(t[k + 1], half, 0)) for k in (0, 2)
                ]
                saved.append(jnp.stack(pairs + [t[4]]))
            for v in range(6):
                extra = pert[PAIR[v, 0], i, j] * saved[0]
                for w in range(1, 6):
                    extra = extra + pert[PAIR[v, w], i, j] * saved[w]
                apart = []
                for k in range(5):
                    held = extra[k // 2]
                    apart.append(jnp.where(upper, 0.0, pltpu.roll(held, half, 0) if k % 2 == 0 else held))
                out[v] = out[v] + jnp.stack(apart)
            s_xx, s_yy, s_zz, s_yz, s_xz, s_xy = out
            for c, value in enumerate((s_xz, s_yz, s_zz)):
                done = backward([value[k] for k in range(5)])
                for k in range(5):
                    force[c, i, j, k] = done[k]
            for place, value in enumerate((s_xx, s_xy, s_xz, s_yy, s_yz)):
                stress[place, i, j] = value

        def face_stresses(line, inner):
            stresses(line // 5 * 4, line % 5)
            return inner
        lax.fori_loop(0, 10, face_stresses, 0)

        def force_y(c, i):
            place = 1 + c + jnp.minimum(c, 1)
            out = backward([stress[place, i, j] for j in range(5)])
            for j in range(5):
                force[c, i, j] = force[c, i, j] + out[j]

        def face_force_y(line, inner):
            force_y(line // 2, line % 2 * 4)
            return inner
        lax.fori_loop(0, 6, face_force_y, 0)

        def inner_stresses(j):
            def one(i, inner):
                stresses(i, j)
                return inner
            lax.fori_loop(1, 4, one, 0)

        def face_row(c, j):
            ends = backward_ends([stress[c, i, j] for i in range(5)])
            return [force[c, side_plane[side], j] + ends[side] for side in range(2)]

        def keep_row(c, side, j, row):
            out = assemble_z(row)
            for k in range(5):
                force[c, side_plane[side], j, k] = out[k]
                if j < 4 and k < 4:
                    rows_out[side, j, c, k] = out[k]

        inner_stresses(0)
        inner_stresses(4)

        def outer_rows(c, inner):
            first, last = face_row(c, 0), face_row(c, 4)
            for side in range(2):
                new_first, new_last = assemble_y(first[side], last[side])
                keep_row(c, side, 0, new_first)
                keep_row(c, side, 4, new_last)
            return inner
        lax.fori_loop(0, 3, outer_rows, 0)
        send_face(slot, 0)

        for j in range(1, 4):
            inner_stresses(j)

            def middle_rows(c, inner, j=j):
                row = face_row(c, j)
                for side in range(2):
                    keep_row(c, side, j, row[side])
                return inner
            lax.fori_loop(0, 3, middle_rows, 0)
            send_face(slot, j)

        for side in range(2):
            i = side_plane[side]
            ends = jnp.zeros(tile, jnp.float32)
            for c in range(3):
                rim = jnp.zeros(tile, jnp.float32)
                for k in range(4):
                    moved = pltpu.roll(force[c, i, 4, k], (k - 3) % 8, 0)
                    rim = jnp.where(y_elem == k, moved, rim)
                rims_out[side, c] = rim
                for j in range(5):
                    moved = pltpu.roll(force[c, i, j, 4], c * 8 + j + 1, 1)
                    ends = jnp.where(z_elem == c * 8 + j, moved, ends)
            rims_out[side, 3] = ends
        send_face(slot, 4)

        def inside_force_y(line, inner):
            force_y(line // 3, 1 + line % 3)
            return inner
        lax.fori_loop(0, 9, inside_force_y, 0)

        def inside_force_x(line, inner):
            c, j = line // 5, line % 5
            out = backward([stress[c, i, j] for i in range(5)])
            for i in range(1, 4):
                force[c, i, j] = force[c, i, j] + out[i]
            return inner
        lax.fori_loop(0, 15, inside_force_x, 0)

        def inside(line, inner):
            c, i = line // 3, 1 + line % 3
            out = assemble_plane([force[c, i, j] for j in range(5)])
            for j in range(5):
                move(c, i, j, jnp.stack(out[j]))
            return inner
        lax.fori_loop(0, 9, inside, 0)

        def inside_y(i, inner):
            along_y(i)
            return inner
        lax.fori_loop(1, 4, inside_y, 0)

        for side in range(2):
            @pl.when(has[side])
            def _(side=side):
                for item in range(5):
                    face_copy(slot, side, item, side).wait()

            i = side_plane[side]
            ends = rims_in[slot, side, 3]
            for c in range(3):
                rim = rims_in[slot, side, c]
                for j in range(5):
                    if j < 4:
                        row = [rows_in[slot, side, j, c, k] for k in range(4)]
                    else:
                        row = [
                            jnp.where(
                                y_elem < 3,
                                pltpu.roll(rows_in[slot, side, 0, c, k], 7, 0),
                                pltpu.roll(rim, 3 - k, 0) if k < 3 else rim,
                            )
                            for k in range(4)
                        ]
                    row.append(
                        jnp.where(
                            z_elem < last_z,
                            pltpu.roll(row[0], last_z, 1),
                            pltpu.roll(ends, last_z - c * 8 - j, 1),
                        )
                    )
                    move(c, i, j, force[c, i, j] + jnp.stack(row))
            along_y(i)

        for c in range(3):
            centre = disp[c, 2, 2, 2]
            for y in range(half):
                records[y, pl.ds((step_id % per_group) * 3 + c, 1)] = centre[half + y : half + y + 1]
        return carry

    def run_group(group, carry):
        lax.fori_loop(group * per_group, (group + 1) * per_group, step, 0)
        send_traces(group)
        return carry
    lax.fori_loop(0, groups, run_group, 0)

    def gather_group(group, carry):
        def add(away, total):
            to_station(group, away).wait()
            return total + inbox[group, away]
        traces[group] = lax.fori_loop(1, count, add, outbox[group, 0])
        return carry
    lax.fori_loop(0, groups, gather_group, 0)


def on_device(
    background_displacement,
    background_velocity,
    born_displacement,
    born_velocity,
    lame_first,
    lame_shear,
    density,
    perturbation,
    station_element,
):
    count = lax.axis_size("slab")
    y_count, z_count = density.shape[4:]
    weight = jnp.asarray(WEIGHT, jnp.float32)[:, :, :, None, None]

    mass, lam, shear = [weight * a[:, :, :, 0] for a in (density, lame_first, lame_shear)]
    pert = weight * perturbation[:, :, :, :, 0].astype(jnp.float32)
    pert = jnp.pad(pert, ((0, 0),) * 3 + ((0, 1), (0, 0), (0, 0)))
    pert = pert.reshape(21, 5, 5, 3, 2 * y_count, z_count)
    starts = [
        a[:, :, :, :, 0]
        for a in (background_displacement, background_velocity, born_displacement, born_velocity)
    ]
    elements_here = y_count * z_count
    owned_count = station_element.shape[0] // count
    element_ids = lax.axis_index("slab") * elements_here + jnp.arange(
        elements_here, dtype=jnp.int32
    )
    chosen = (
        station_element.reshape(count, 1, owned_count) == element_ids[None, :, None]
    ).astype(jnp.bfloat16)
    groups = 4
    rows = -(-(STEPS // groups * 3) // 16) * 16

    cube = (5, 5, 5, 2 * y_count, z_count)
    face = (5, 5, 2 * y_count, z_count)
    vmem = pl.BlockSpec(memory_space=pltpu.VMEM)
    disp, traces = pl.pallas_call(
        lambda *refs: kernel(count, *refs),
        out_shape=(
            jax.ShapeDtypeStruct((3,) + cube, jnp.float32),
            jax.ShapeDtypeStruct((groups, rows, owned_count), jnp.float32),
        ),
        in_specs=[vmem] * 9,
        out_specs=(vmem, vmem),
        scratch_shapes=[
            pltpu.VMEM((3,) + cube, jnp.float32),
            pltpu.VMEM(cube, jnp.float32),
            pltpu.VMEM(cube, jnp.float32),
            pltpu.VMEM(cube, jnp.float32),
            pltpu.VMEM((3,) + cube, jnp.float32),
            pltpu.VMEM((3,) + cube, jnp.float32),
            pltpu.VMEM((5,) + cube, jnp.float32),
            pltpu.VMEM((3,) + cube, jnp.float32),
            pltpu.VMEM((2, 4, 3, 4) + cube[3:], jnp.float32),
            pltpu.VMEM((2, 4) + cube[3:], jnp.float32),
            pltpu.VMEM((2, 2, 4, 3, 4) + cube[3:], jnp.float32),
            pltpu.VMEM((2, 2, 4) + cube[3:], jnp.float32),
            pltpu.VMEM((2, 7) + face, jnp.float32),
            pltpu.VMEM((y_count, rows, z_count), jnp.float32),
            pltpu.VMEM((groups, count, rows, owned_count), jnp.float32),
            pltpu.VMEM((groups, count, rows, owned_count), jnp.float32),
            pltpu.SemaphoreType.DMA((2, 5)),
            pltpu.SemaphoreType.DMA((2, 2, 5)),
            pltpu.SemaphoreType.DMA((2, 7)),
            pltpu.SemaphoreType.DMA((2, 7)),
            pltpu.SemaphoreType.DMA((groups, count)),
            pltpu.SemaphoreType.DMA((groups, count)),
        ],
        compiler_params=pltpu.CompilerParams(
            collective_id=0, has_side_effects=True, vmem_limit_bytes=56 * 1024 * 1024
        ),
        name="born_window",
    )(*starts, mass, lam, shear, pert, chosen)

    back_disp = disp[:, :, :, :, None, :y_count]
    born_disp = disp[:, :, :, :, None, y_count:]
    station_traces = traces[:, : STEPS // groups * 3].reshape(STEPS, 3, owned_count)
    station_traces = station_traces.transpose(1, 0, 2)
    return (back_disp, born_disp, station_traces)


def solution(mesh):
    placed = (
        P("shot", None, None, None, "slab", None, None),
        P("shot", None, None, None, "slab", None, None),
        P("shot", None, None, None, "slab", None, None),
        P("shot", None, None, None, "slab", None, None),
        P(None, None, None, "slab", None, None),
        P(None, None, None, "slab", None, None),
        P(None, None, None, "slab", None, None),
        P("shot", None, None, None, "slab", None, None),
        P(),
    )
    return jax.shard_map(
        on_device,
        mesh=mesh,
        in_specs=placed,
        out_specs=(
            P("shot", None, None, None, "slab", None, None),
            P("shot", None, None, None, "slab", None, None),
            P("shot", None, "slab"),
        ),
        check_vma=False,
    )
```
